256 devices in a mesh: section: 32 (over y, z), group: 8 (over x, core).
Axes of the slice: x: 4, y: 4, z: 8, core: 2. Of those that a mesh axis runs over, the one named last changes fastest.
Arguments:
- query_rows: bfloat16 [16384, 8192], P('section', 'group'), may hold values from -6 to 6
- key_rows: bfloat16 [16384, 8192], P('section', 'group'), may hold values from -6 to 6
- value_rows: bfloat16 [16384, 8192], P('section', 'group'), may hold values from -6 to 6
- log_decay: float32 [16384, 64], P('section', 'group'), may hold values from -1 to 0
- norm_gain: float32 [8192], P('group'), may hold values from 0.1 to 1.9
- out_proj: bfloat16 [8192, 6144], P('group', 'section'), may hold values from -0.0625 to 0.0625
Outputs:
- mixed: bfloat16 [16384, 6144], P('section', 'group')
The draws below stay inside these ranges and needn't reach their ends.
All inputs are finite; a program needn't handle non-finite values.
Results may differ from the reference program's by a relative error of at most 0.015.
Values may be sent and summed in bfloat16 or wider, within the bound.
A program may use at most 128 MiB of HBM per device.

```python
import math
import jax
import jax.numpy as jnp
from jax import lax

D = 6144
HEADS = 64
HD = 128
BLOCK = 512
SEQUENCE_TOKENS = 16384
N_GROUP = 8


def draw_log_decay(key, part):
    key = jax.random.fold_in(key, 7)
    key_inputs = jax.random.split(key, 7)
    share = 0.5
    pick = jax.random.uniform(key_inputs[0], (HEADS,))
    fast_rate = jnp.exp(jax.random.uniform(key_inputs[1], (HEADS,), minval=math.log(1.0 / 50.0), maxval=math.log(1.0 / 25.0)))
    slow_rate = jnp.exp(jax.random.uniform(key_inputs[2], (HEADS,), minval=math.log(0.05 / SEQUENCE_TOKENS), maxval=math.log(0.5 / SEQUENCE_TOKENS)))
    decay_speed = jnp.where(pick < share, fast_rate, slow_rate)
    block_decay_factor = jnp.exp(jax.random.uniform(key_inputs[3], (SEQUENCE_TOKENS // BLOCK, HEADS), minval=-math.log(2.0), maxval=math.log(2.0)))
    block_decay_factor = jnp.repeat(block_decay_factor, BLOCK, axis=0)
    position_decay_factor = jnp.exp(jax.random.uniform(key_inputs[4], (SEQUENCE_TOKENS, HEADS), minval=-math.log(2.0), maxval=math.log(2.0)))
    segment_offsets = jax.random.randint(key_inputs[5], (2,), 0, SEQUENCE_TOKENS)
    segment_lengths = jax.random.uniform(key_inputs[6], (2,), minval=0.22, maxval=0.51)
    token_positions = jnp.arange(SEQUENCE_TOKENS)
    segment_spans = jnp.sum(jnp.where(token_positions[:, None] == segment_offsets[None, :], segment_lengths[None, :], 0.0), axis=1)
    return (-(decay_speed[None, :] * block_decay_factor * position_decay_factor) - segment_spans[:, None]).astype(jnp.float32)


def level_of(own_key, extent, shards, low, top_value):
    factor_of = 1.0
    for dim, shards_of in shards:
        draws = jax.random.uniform(jax.random.fold_in(jax.random.fold_in(own_key, 6), dim), (shards_of,), jnp.float32, low / len(shards), top_value / len(shards))
        factor_of = factor_of * jnp.repeat(jnp.exp(draws), extent[dim] // shards_of).reshape((-1,) + (1,) * (len(extent) - 1 - dim))
    return factor_of


def bell_draw(key, dims, scale, reach, shards=(), kind=jnp.bfloat16):
    drawn = scale * jax.random.normal(key, dims, jnp.float32)
    if shards:
        drawn = drawn * level_of(key, dims, shards, -0.22, 0.18)
    return jnp.clip(drawn, -reach, reach).astype(kind)


def setup_inputs(seed: int = 0) -> dict:
    seeds = jax.random.split(jax.random.key(seed), 7)
    query_rows = bell_draw(seeds[0], (SEQUENCE_TOKENS, HEADS * HD), 1.0, 6.0, ((0, 32), (1, 8)))
    key_rows = bell_draw(seeds[1], (SEQUENCE_TOKENS, HEADS * HD), 1.0, 6.0, ((0, 32), (1, 8)))
    value_rows = bell_draw(seeds[2], (SEQUENCE_TOKENS, HEADS * HD), 1.0, 6.0, ((0, 32), (1, 8)))
    log_decay = draw_log_decay(jax.random.fold_in(seeds[6], 71), 0)
    norm_gain = jnp.clip(1.0 + 0.18 * jax.random.normal(seeds[4], (HEADS * HD,), jnp.float32), 0.1, 1.9)
    out_proj = bell_draw(seeds[5], (HEADS * HD, D), (HEADS * HD) ** -0.5, 0.0625, ((0, 8), (1, 32)))
    return dict(query_rows=query_rows, key_rows=key_rows, value_rows=value_rows, log_decay=log_decay, norm_gain=norm_gain, out_proj=out_proj)


def span_core(query, key, value, decay):
    cumul = jnp.cumsum(decay, axis=0)
    total = cumul[-1]
    scores = jnp.einsum('thd,shd->hts', query.astype(jnp.float32), key.astype(jnp.float32))
    length = decay.shape[0]
    token_positions = jnp.arange(length)
    causal = (token_positions[:, None] >= token_positions[None, :])[None]
    spread = cumul.T[:, :, None] - cumul.T[:, None, :]
    factor = jnp.where(causal, jnp.exp(jnp.where(causal, spread, 0.0)), 0.0)
    weights = (scores * factor).astype(jnp.bfloat16)
    intra = jnp.einsum('hts,she->the', weights.astype(jnp.float32), value.astype(jnp.float32))
    scaled_keys = key.astype(jnp.float32) * jnp.exp(total[None, :] - cumul)[:, :, None]
    update = jnp.einsum('shd,she->hde', scaled_keys, value.astype(jnp.float32), precision=lax.Precision.HIGHEST)
    return (intra, cumul, total, update)

def normalize(attended, gain):
    moment = lax.optimization_barrier(jnp.mean(attended * attended, axis=-1, keepdims=True))
    return (attended * lax.rsqrt(moment + 1e-06) * gain).astype(jnp.bfloat16)

def reference(query_rows, key_rows, value_rows, log_decay, norm_gain, out_proj):
    blocks = SEQUENCE_TOKENS // BLOCK
    query_all = query_rows.reshape(blocks, BLOCK, HEADS, HD)
    key_all = key_rows.reshape(blocks, BLOCK, HEADS, HD)
    value_all = value_rows.reshape(blocks, BLOCK, HEADS, HD)
    decay_all = log_decay.reshape(blocks, BLOCK, HEADS)
    gain = norm_gain.reshape(HEADS, HD)

    def advance(state, pieces):
        query, key, value, decay = pieces
        intra, cumul, total, update = span_core(query, key, value, decay)
        lifted = query.astype(jnp.float32) * jnp.exp(cumul)[:, :, None]
        inter = jnp.einsum('thd,hde->the', lifted, state, precision=lax.Precision.HIGHEST)
        normed = normalize(intra + inter, gain)
        state_next = jnp.exp(total)[:, None, None] * state + update
        return (state_next, normed)
    start = jnp.zeros((HEADS, HD, HD), jnp.float32)
    final_state, normed = lax.scan(advance, start, (query_all, key_all, value_all, decay_all))
    normed = normed.reshape(SEQUENCE_TOKENS, HEADS * HD)
    group_width = HEADS * HD // N_GROUP
    summed = jnp.zeros((SEQUENCE_TOKENS, D), jnp.float32)
    for index in range(N_GROUP):
        left = normed[:, index * group_width:(index + 1) * group_width]
        right = out_proj[index * group_width:(index + 1) * group_width]
        partial_sum = jnp.dot(left, right, preferred_element_type=jnp.float32).astype(jnp.bfloat16)
        summed = summed + partial_sum.astype(jnp.float32)
    return summed.astype(jnp.bfloat16)
```

```python
import functools

import jax
import jax.numpy as jnp
from jax import lax
from jax.experimental import pallas as pl
from jax.experimental.pallas import tpu as pltpu
from jax.sharding import PartitionSpec as P

BF = jnp.bfloat16
F32 = jnp.float32
MESH = pl.DeviceIdType.MESH
TOK = 512
HALF = 256
HEADS = 8
HD = 128
WIDTH = HEADS * HD
PIECE = 192
CUT = 96
NY, NZ, NX, NS = 4, 8, 4, 32
SLOT = 48
PART = 32
STEPS = (0, -1, 1, 2)
ROWS = (0, 1, -1, 2)


def nt(a, b):
    return lax.dot_general(a, b, (((1,), (1,)), ((), ())), preferred_element_type=F32)


def tn(a, b):
    return lax.dot_general(a, b, (((0,), (0,)), ((), ())), preferred_element_type=F32)


def nn(a, b):
    return jnp.dot(a, b, preferred_element_type=F32)


def kernel(
    q_hbm, k_hbm, v_hbm, w_hbm, decay_ref, gain_ref, out_hbm,
    qb, kb, vb, wraw, wb, ab, intra, colc, rowc, ust, urecv, pst, precv, factor,
    dbuf, fbuf, xrecv, fin, otb,
    load_sem, out_sem, wz_s, wz_r, wy_s, wy_r, st_s, st_r, a_s, a_r, d_s, d_r, x_s, x_r, b_s, b_r,
):
    sec = lax.axis_index("section")
    grp = lax.axis_index("group")
    y, z = sec // NZ, lax.rem(sec, NZ)
    x, c = grp // 2, lax.rem(grp, 2)
    h, k0 = lax.rem(z, 2), z // 2

    def at(dy, dz):
        return (lax.rem(y + dy + NY, NY) * NZ + lax.rem(z + dz + NZ, NZ), grp)

    mate = (sec, x * 2 + 1 - c)

    def along_x(xx):
        return (sec, xx * 2 + c)

    def remote(src, dst, ssem, rsem, dev):
        return pltpu.make_async_remote_copy(
            src_ref=src, dst_ref=dst, send_sem=ssem, recv_sem=rsem, device_id=dev, device_id_type=MESH
        )

    loads = [
        pltpu.make_async_copy(s, d, load_sem.at[i])
        for i, (s, d) in enumerate(((w_hbm, wraw), (k_hbm, kb), (v_hbm, vb), (q_hbm, qb)))
    ]
    for cp in loads:
        cp.start()
    bar = pltpu.get_barrier_semaphore()

    def greet(i, _):
        pl.semaphore_signal(bar, inc=1, device_id=(lax.rem(sec + i, NS), grp), device_id_type=MESH)
        return 0

    lax.fori_loop(1, NS, greet, 0)
    pl.semaphore_signal(bar, inc=1, device_id=mate, device_id_type=MESH)
    for i in range(1, NX):
        pl.semaphore_signal(bar, inc=1, device_id=along_x(lax.rem(x + i, NX)), device_id_type=MESH)

    d = jnp.concatenate([decay_ref[...], jnp.zeros((TOK, HD - HEADS), F32)], axis=1)
    hi = d.astype(BF)
    rest = d - hi.astype(F32)
    mid = rest.astype(BF)
    low = (rest - mid.astype(F32)).astype(BF)
    tri = (
        lax.broadcasted_iota(jnp.int32, (TOK, TOK), 0) >= lax.broadcasted_iota(jnp.int32, (TOK, TOK), 1)
    ).astype(F32).astype(BF)
    cum = nn(tri, hi) + (nn(tri, mid) + nn(tri, low))
    colc[...] = cum
    rowc[...] = cum.T[0:HEADS]

    loads[0].wait()
    wb[y, k0] = wraw[...].T
    pl.semaphore_wait(bar, NS - 1 + 1 + NX - 1)

    def wz(i):
        if i < 2:
            ref = wb.at[y, k0]
            dz = 2 if i == 0 else -2
        elif i == 2:
            ref = wb.at[y, lax.rem(k0 + 3, 4), pl.ds(0, CUT)]
            dz = 2
        else:
            ref = wb.at[y, lax.rem(k0 + 1, 4), pl.ds(CUT, CUT)]
            dz = -2
        return remote(ref, ref, wz_s.at[i], wz_r.at[i], at(0, dz))

    def wz_wait(i):
        if i < 2:
            ref = wb.at[y, lax.rem(k0 + (3 if i == 0 else 1), 4)]
        else:
            ref = wb.at[y, lax.rem(k0 + 2, 4), pl.ds(0 if i == 2 else CUT, CUT)]
        remote(ref, ref, wz_s.at[i], wz_r.at[i], at(0, 0)).wait_recv()

    def kq(q):
        return lax.rem(k0 + STEPS[q] + 4, 4)

    def wy(q, i):
        if i < 2:
            ref = wb.at[y, kq(q)]
            dy = 1 if i == 0 else -1
        elif i == 2:
            ref = wb.at[lax.rem(y + 3, NY), kq(q), pl.ds(0, CUT)]
            dy = 1
        else:
            ref = wb.at[lax.rem(y + 1, NY), kq(q), pl.ds(CUT, CUT)]
            dy = -1
        return remote(ref, ref, wy_s.at[q, i], wy_r.at[q, i], at(dy, 0))

    def wy_wait(q, i):
        if i < 2:
            ref = wb.at[lax.rem(y + (3 if i == 0 else 1), NY), kq(q)]
        else:
            ref = wb.at[lax.rem(y + 2, NY), kq(q), pl.ds(0 if i == 2 else CUT, CUT)]
        remote(ref, ref, wy_s.at[q, i], wy_r.at[q, i], at(0, 0)).wait_recv()

    def y_send(q):
        wy(q, 0).start()
        wy(q, 1).start()

    def y_forward(q):
        wy_wait(q, 0)
        wy(q, 2).start()
        wy_wait(q, 1)
        wy(q, 3).start()

    wz(0).start()
    wz(1).start()
    y_send(0)

    loads[1].wait()
    loads[2].wait()
    total = rowc[:, TOK - 1:TOK] + jnp.zeros((HEADS, HD), F32)
    total_hi = total.astype(BF)
    total_lo = (total - total_hi.astype(F32)).astype(BF)
    tail = jnp.concatenate([total_hi.astype(F32), total_lo.astype(F32)], axis=0).astype(BF)
    for j in range(NS):
        ust[j, PART:SLOT] = tail
    for i in range(HEADS):
        col = colc[:, i:i + 1]
        last = colc[TOK - 1:TOK, i:i + 1]
        keys = (kb[:, i * HD:(i + 1) * HD].astype(F32) * jnp.exp(last - col)).astype(BF)
        upd = tn(keys, vb[:, i * HD:(i + 1) * HD]).astype(BF)
        for j in range(4):
            ust[4 * i + j, 0:PART] = upd[j * PART:(j + 1) * PART]

    def send_update(i, _):
        to = lax.rem(sec + i, NS)
        remote(ust.at[to], urecv.at[sec], st_s.at[0], st_r.at[0], (to, grp)).start()
        return 0

    lax.fori_loop(1, NS, send_update, 0)
    urecv[sec] = ust[sec]

    loads[3].wait()
    causal = lax.broadcasted_iota(jnp.int32, (HALF, HALF), 0) >= lax.broadcasted_iota(jnp.int32, (HALF, HALF), 1)

    def inside(i):
        cols = slice(i * HD, (i + 1) * HD)
        for b in range(2):
            rows = slice(b * HALF, (b + 1) * HALF)
            qt = qb[rows, cols]
            col = colc[rows, i:i + 1]
            acc = None
            for e in range(b + 1):
                sl = slice(e * HALF, (e + 1) * HALF)
                scores = nt(qt, kb[sl, cols])
                spread = col - rowc[i:i + 1, sl]
                if e == b:
                    spread = jnp.where(causal, spread, -1e30)
                weights = (scores * jnp.exp(spread)).astype(BF)
                term = nn(weights, vb[sl, cols])
                acc = term if acc is None else acc + term
            intra[rows, cols] = acc

    for i in range(4):
        inside(i)
    y_forward(0)

    head = sec // 4
    whole = pl.ds(0, NS - 1)
    remote(ust.at[whole], urecv.at[whole], st_s.at[0], st_r.at[0], at(0, 0)).wait_recv()
    pick = lax.rem(lax.broadcasted_iota(jnp.int32, (NS, SLOT - PART, HD), 1), HEADS) == head
    logs = jnp.sum(jnp.where(pick, urecv[:, PART:SLOT, :].astype(F32), 0.0), axis=1)
    factor[...] = jnp.exp(logs)
    state = jnp.zeros((PART, HD), F32)
    for j in range(NS):
        pst[j] = state.astype(BF)
        if j < NS - 1:
            state = state * factor[j:j + 1, :] + urecv[j, 0:PART, :].astype(F32)

    def send_state(i, _):
        to = lax.rem(sec + i, NS)
        remote(pst.at[to], precv.at[sec], st_s.at[1], st_r.at[1], (to, grp)).start()
        return 0

    lax.fori_loop(1, NS, send_state, 0)
    precv[sec] = pst[sec]

    for i in range(4, HEADS):
        inside(i)
    wz_wait(0)
    wz(2).start()
    wz_wait(1)
    wz(3).start()
    y_send(1)
    y_send(2)

    remote(pst.at[whole], precv.at[whole], st_s.at[1], st_r.at[1], at(0, 0)).wait_recv()

    def a_send(i):
        src = ab.at[pl.ds(i * HALF, HALF)]
        dst = ab.at[pl.ds(TOK + i * HALF, HALF)]
        return remote(src, dst, a_s.at[i], a_r.at[i], at(0, -1 if i == 0 else 1))

    for i in range(HEADS):
        cols = slice(i * HD, (i + 1) * HD)
        carried = precv[4 * i:4 * i + 4].reshape(HD, HD)
        att = intra[:, cols] + jnp.exp(colc[:, i:i + 1]) * nn(qb[:, cols], carried)
        moment = jnp.mean(att * att, axis=1, keepdims=True)
        ab[0:TOK, cols] = (att * lax.rsqrt(moment + 1e-6) * gain_ref[i:i + 1, :]).astype(BF)
    a_send(0).start()
    a_send(1).start()

    def names(q, r):
        yy = lax.rem(y + ROWS[r] + NY, NY)
        k = kq(q)
        return yy, k, (k // 2) == c, lax.rem(k, 2)

    def mate_copy(n):
        return remote(dbuf.at[n], dbuf.at[n], d_s.at[n], d_r.at[n], mate)

    def x_copy(n, yy, kk, half):
        return remote(dbuf.at[n], xrecv.at[x, kk, half], x_s.at[n], x_r.at[x, kk, half], along_x(yy))

    def compute(n, unit):
        q, r, half = unit
        yy, k, mine, kk = names(q, r)
        res = nt(wb[yy, k], ab[half * TOK:(half + 1) * TOK])

        @pl.when(mine)
        def _():
            fbuf[n % 2] = res

        @pl.when(jnp.logical_not(mine))
        def _():
            dbuf[n] = res.astype(BF)
            mate_copy(n).start()

    def finish(n, unit):
        q, r, half = unit
        yy, k, mine, kk = names(q, r)

        @pl.when(mine)
        def _():
            mate_copy(n).wait_recv()
            val = (fbuf[n % 2] + dbuf[n].astype(F32)).astype(BF)

            @pl.when(yy == x)
            def _():
                xrecv[x, kk, half] = val

            @pl.when(yy != x)
            def _():
                dbuf[n] = val
                x_copy(n, yy, kk, half).start()

    order = []

    def add(q, rows, half):
        order.extend([(q, r, half) for r in rows])

    hooks = {}

    def hook(fn):
        hooks.setdefault(len(order), []).append(fn)

    def z_last():
        wz_wait(2)
        wz_wait(3)
        y_send(3)

    def a_wait():
        for i in range(2):
            a_send(i).wait_recv()

    add(0, (0, 1, 2), 0)
    hook(lambda: (wy_wait(0, 2), wy_wait(0, 3)))
    add(0, (3,), 0)
    add(1, (0,), 0)
    add(2, (0,), 0)
    hook(z_last)
    hook(lambda: y_forward(1))
    add(1, (1, 2), 0)
    hook(a_wait)
    add(0, (0, 1, 2, 3), 1)
    hook(lambda: y_forward(2))
    add(1, (0, 1, 2), 1)
    hook(lambda: (wy_wait(1, 2), wy_wait(1, 3)))
    add(1, (3,), 0)
    add(1, (3,), 1)
    add(2, (1, 2), 0)
    add(2, (0, 1, 2), 1)
    add(3, (0,), 0)
    add(3, (0,), 1)
    hook(lambda: (wy_wait(2, 2), wy_wait(2, 3)))
    add(2, (3,), 0)
    add(2, (3,), 1)
    hook(lambda: y_forward(3))
    add(3, (1, 2), 0)
    add(3, (1, 2), 1)
    hook(lambda: (wy_wait(3, 2), wy_wait(3, 3)))
    add(3, (3,), 0)
    add(3, (3,), 1)

    for n, unit in enumerate(order):
        for fn in hooks.get(n, ()):
            fn()
        compute(n, unit)
        if n:
            finish(n - 1, order[n - 1])
    finish(len(order) - 1, order[-1])

    def back(kk, i):
        src = fin.at[kk, :, pl.ds(i * HALF, HALF)]
        dst = otb.at[2 * kk + h, :, pl.ds(i * HALF, HALF)]
        return remote(src, dst, b_s.at[kk, i], b_r.at[kk, i], at(0, 1 if i == 0 else -1))

    def back_wait(kk, i):
        ref = otb.at[2 * kk + 1 - h, :, pl.ds(i * HALF, HALF)]
        remote(ref, ref, b_s.at[kk, i], b_r.at[kk, i], at(0, 0)).wait_recv()

    def total_of(kk, half):
        for i in range(1, NX):
            xs = lax.rem(x + i, NX)
            remote(dbuf.at[0], xrecv.at[xs, kk, half], x_s.at[0], x_r.at[xs, kk, half], mate).wait_recv()
        acc = xrecv[0, kk, half].astype(F32) + xrecv[1, kk, half].astype(F32)
        acc = acc + (xrecv[2, kk, half].astype(F32) + xrecv[3, kk, half].astype(F32))
        return acc.astype(BF)

    for kk in range(2):
        fin[kk] = total_of(kk, 1)
        back(kk, 0).start()
        back(kk, 1).start()
    for kk in range(2):
        otb[2 * kk + h] = total_of(kk, 0)
    for kk in range(2):
        for i in range(2):
            back_wait(kk, i)
    final = pltpu.make_async_copy(otb, out_hbm, out_sem.at[0])
    final.start()

    for i in range(4):
        wz(i).wait_send()
    for q in range(4):
        for i in range(4):
            wy(q, i).wait_send()
    for i in range(2):
        a_send(i).wait_send()
    remote(ust.at[whole], urecv.at[whole], st_s.at[0], st_r.at[0], at(0, 0)).wait_send()
    remote(pst.at[whole], precv.at[whole], st_s.at[1], st_r.at[1], at(0, 0)).wait_send()
    for n, (q, r, half) in enumerate(order):
        yy, k, mine, kk = names(q, r)

        @pl.when(jnp.logical_and(mine, yy != x))
        def _():
            x_copy(n, yy, kk, half).wait_send()

        @pl.when(jnp.logical_not(mine))
        def _():
            mate_copy(n).wait_send()

    for kk in range(2):
        for i in range(2):
            back(kk, i).wait_send()
    final.wait()


def shards(query_rows, key_rows, value_rows, log_decay, norm_gain, out_proj):
    vmem = pltpu.VMEM
    dma = pltpu.SemaphoreType.DMA
    anywhere = pl.BlockSpec(memory_space=pl.ANY)
    near = pl.BlockSpec(memory_space=pltpu.VMEM)
    out = pl.pallas_call(
        kernel,
        name="parity_attention",
        out_shape=jax.ShapeDtypeStruct((4, PIECE, TOK), BF),
        in_specs=[anywhere] * 4 + [near] * 2,
        out_specs=anywhere,
        scratch_shapes=[
            vmem((TOK, WIDTH), BF),
            vmem((TOK, WIDTH), BF),
            vmem((TOK, WIDTH), BF),
            vmem((WIDTH, PIECE), BF),
            vmem((NY, 4, PIECE, WIDTH), BF),
            vmem((2 * TOK, WIDTH), BF),
            vmem((TOK, WIDTH), F32),
            vmem((TOK, HD), F32),
            vmem((HEADS, TOK), F32),
            vmem((NS, SLOT, HD), BF),
            vmem((NS, SLOT, HD), BF),
            vmem((NS, PART, HD), BF),
            vmem((NS, PART, HD), BF),
            vmem((NS, HD), F32),
            vmem((32, PIECE, TOK), BF),
            vmem((2, PIECE, TOK), F32),
            vmem((NX, 2, 2, PIECE, TOK), BF),
            vmem((2, PIECE, TOK), BF),
            vmem((4, PIECE, TOK), BF),
            dma((4,)),
            dma((1,)),
            dma((4,)),
            dma((4,)),
            dma((4, 4)),
            dma((4, 4)),
            dma((2,)),
            dma((2,)),
            dma((2,)),
            dma((2,)),
            dma((32,)),
            dma((32,)),
            dma((32,)),
            dma((NX, 2, 2)),
            dma((2, 2)),
            dma((2, 2)),
        ],
        compiler_params=pltpu.CompilerParams(
            collective_id=0, has_side_effects=True, vmem_limit_bytes=56 * 2**20
        ),
        cost_estimate=pl.CostEstimate(flops=8 * 10**9, bytes_accessed=5 * 2**20, transcendentals=2 * 10**6),
    )(query_rows, key_rows, value_rows, out_proj, log_decay, norm_gain.reshape(HEADS, HD))
    return out.reshape(4 * PIECE, TOK).T


def solution(mesh):
    return jax.shard_map(
        shards,
        mesh=mesh,
        in_specs=(
            P("section", "group"),
            P("section", "group"),
            P("section", "group"),
            P("section", "group"),
            P("group"),
            P("group", "section"),
        ),
        out_specs=P("section", "group"),
        check_vma=False,
    )
```

```python
import functools

import jax
import jax.numpy as jnp
from jax import lax
from jax.experimental import pallas as pl
from jax.experimental.pallas import tpu as pltpu
from jax.sharding import PartitionSpec as P

BF = jnp.bfloat16
F32 = jnp.float32
MESH = pl.DeviceIdType.MESH
TOK = 512
HALF = 256
HEADS = 8
HD = 128
WIDTH = HEADS * HD
PIECE = 192
CUT = 96
CHUNK = 48
CHUNKS = (0, 2, 1, 3)
NY, NZ, NX = 4, 8, 4
SLOT = HD + 16


def nt(a, b):
    return lax.dot_general(a, b, (((1,), (1,)), ((), ())), preferred_element_type=F32)


def tn(a, b):
    return lax.dot_general(a, b, (((0,), (0,)), ((), ())), preferred_element_type=F32)


def nn(a, b):
    return jnp.dot(a, b, preferred_element_type=F32)


EARLY = {0: (0, 2), 7: (1, 3)}


def fold(i):
    return i + i // 2 - 2 * (i // 3)


def kernel(
    q_hbm, k_hbm, v_hbm, w_hbm, decay_ref, gain_ref, out_hbm,
    qb, kb, vb, wb, ab, intra, colc, rowc, ust, urecv, lst, lead, rst, rrecv, pst, precv,
    dbuf, fbuf, relay, own, xrecv, fin, otb,
    load_sem, out_sem, wz_s, wz_r, wy_s, wy_r, st_s, st_r, row_s, row_r, a_s, a_r, d_s, d_r, x_s, x_r, r_r, b_s, b_r,
):
    sec = lax.axis_index("section")
    grp = lax.axis_index("group")
    y, z = sec // NZ, lax.rem(sec, NZ)
    x, c = grp // 2, lax.rem(grp, 2)
    h, k0 = lax.rem(z, 2), z // 2

    def at(dy, dz):
        return (lax.rem(y + dy + NY, NY) * NZ + lax.rem(z + dz + NZ, NZ), grp)

    mate = (sec, x * 2 + 1 - c)

    def along_x(xx):
        return (sec, xx * 2 + c)

    def remote(src, dst, ssem, rsem, dev):
        return pltpu.make_async_remote_copy(
            src_ref=src, dst_ref=dst, send_sem=ssem, recv_sem=rsem, device_id=dev, device_id_type=MESH
        )

    loads = [
        pltpu.make_async_copy(s, d, load_sem.at[i])
        for i, (s, d) in enumerate(((w_hbm, wb.at[y, k0]), (k_hbm, kb), (v_hbm, vb), (q_hbm, qb)))
    ]
    for cp in loads:
        cp.start()
    bar = pltpu.get_barrier_semaphore()
    peers = [at(0, i) for i in range(1, NZ)] + [at(i, 0) for i in range(1, NY)]
    peers += [along_x(lax.rem(x + i, NX)) for i in (1, 3)] + [mate]
    for dev in peers:
        pl.semaphore_signal(bar, inc=1, device_id=dev, device_id_type=MESH)

    d = decay_ref[...]
    hi = d.astype(BF).astype(F32)
    mid = (d - hi).astype(BF).astype(F32)
    low = d - hi - mid
    tri = (
        lax.broadcasted_iota(jnp.int32, (TOK, TOK), 0) <= lax.broadcasted_iota(jnp.int32, (TOK, TOK), 1)
    ).astype(F32).astype(BF)
    cum = nn(jnp.concatenate([hi, mid, low, jnp.zeros_like(d)], axis=0).astype(BF), tri)
    cum = cum[0:HEADS] + (cum[HEADS:2 * HEADS] + cum[2 * HEADS:3 * HEADS])
    rowc[...] = cum
    colc[...] = jnp.concatenate([cum, jnp.zeros((HD - HEADS, TOK), F32)], axis=0).T

    def two_terms(val):
        top = val.astype(BF).astype(F32)
        return jnp.concatenate([top, val - top], axis=0).astype(BF)

    loads[1].wait()
    loads[2].wait()
    tail = two_terms(cum[:, TOK - 1:TOK] + jnp.zeros((HEADS, HD), F32))
    for i in range(HEADS):
        col = colc[:, i:i + 1]
        last = colc[TOK - 1:TOK, i:i + 1]
        keys = (kb[:, i * HD:(i + 1) * HD].astype(F32) * jnp.exp(last - col)).astype(BF)
        ust[i, 0:HD] = tn(keys, vb[:, i * HD:(i + 1) * HD]).astype(BF)
        ust[i, HD:SLOT] = tail
    loads[0].wait()
    pl.semaphore_wait(bar, len(peers))

    def send_z(src, dst, i):
        def one(o, _):
            to = lax.rem(z + o, NZ)
            remote(src.at[to], dst.at[z], st_s.at[i], st_r.at[i], (y * NZ + to, grp)).start()
            return 0

        lax.fori_loop(1, NZ, one, 0)

    def sent_z(src, dst, i):
        some = pl.ds(0, NZ - 1)
        return remote(src.at[some], dst.at[some], st_s.at[i], st_r.at[i], at(0, 0))

    send_z(ust, urecv, 0)

    def cut(b):
        return pl.ds(b * CUT, CUT)

    def chunk(b):
        return pl.ds(b * CHUNK, CHUNK)

    def kq(q):
        turn = 1 + 2 * lax.rem(k0, 2)
        return lax.rem(k0 + (0, turn, 4 - turn, 2)[q], 4)

    def wz(b, i):
        if i < 2:
            ref = wb.at[y, k0, chunk(b)]
            dz = 2 if i == 0 else -2
        else:
            ref = wb.at[y, lax.rem(k0 + (3 if b < 2 else 1), 4), chunk(b)]
            dz = 2 if b < 2 else -2
        return remote(ref, ref, wz_s.at[b, i], wz_r.at[b, i], at(0, dz))

    def wz_wait(b, i):
        ref = wb.at[y, lax.rem(k0 + (3, 1, 2)[i], 4), chunk(b)]
        remote(ref, ref, wz_s.at[b, i], wz_r.at[b, i], at(0, 0)).wait_recv()

    def wy(q, b, i):
        if i < 2:
            ref = wb.at[y, kq(q), chunk(b)]
            dy = 1 if i == 0 else -1
        else:
            ref = wb.at[lax.rem(y + (3 if b < 2 else 1), NY), kq(q), chunk(b)]
            dy = 1 if b < 2 else -1
        return remote(ref, ref, wy_s.at[q, b, i], wy_r.at[q, b, i], at(dy, 0))

    def wy_wait(q, b, i):
        ref = wb.at[lax.rem(y + (3, 1, 2)[i], NY), kq(q), chunk(b)]
        remote(ref, ref, wy_s.at[q, b, i], wy_r.at[q, b, i], at(0, 0)).wait_recv()

    def y_send(q, b):
        wy(q, b, 0).start()
        wy(q, b, 1).start()

    def y_forward(q, b):
        wy_wait(q, b, b // 2)
        wy(q, b, 2).start()
        wy_wait(q, b, 1 - b // 2)

    def turn(q, bs):
        for b in bs:
            y_forward(q, b)
            if q < 3:
                if q == 2:
                    wz_wait(b, 2)
                y_send(q + 1, b)

    def y_last(q):
        for b in CHUNKS:
            wy_wait(q, b, 2)

    def z_forward(b):
        wz_wait(b, b // 2)
        wz(b, 2).start()
        wz_wait(b, 1 - b // 2)
        y_send(1, b)

    for b in CHUNKS:
        y_send(0, b)

    loads[3].wait()
    causal = lax.broadcasted_iota(jnp.int32, (HALF, HALF), 0) >= lax.broadcasted_iota(jnp.int32, (HALF, HALF), 1)

    def inside(i):
        cols = slice(i * HD, (i + 1) * HD)
        for b in range(2):
            rows = slice(b * HALF, (b + 1) * HALF)
            qt = qb[rows, cols]
            col = colc[rows, i:i + 1]
            acc = None
            for e in range(b + 1):
                sl = slice(e * HALF, (e + 1) * HALF)
                scores = nt(qt, kb[sl, cols])
                spread = col - rowc[i:i + 1, sl]
                if e == b:
                    spread = jnp.where(causal, spread, -1e30)
                weights = (scores * jnp.exp(spread)).astype(BF)
                term = nn(weights, vb[sl, cols])
                acc = term if acc is None else acc + term
            intra[rows, cols] = acc

    for i in range(HEADS):
        inside(i)
        if i in EARLY:
            for b in EARLY[i]:
                wz(b, 0).start()
                wz(b, 1).start()

    urecv[z] = ust[z]
    for b in CHUNKS:
        y_forward(0, b)
    sent_z(ust, urecv, 0).wait_recv()
    pick = lax.rem(lax.broadcasted_iota(jnp.int32, (NZ, SLOT - HD, HD), 1), HEADS) == z
    logs = jnp.sum(jnp.where(pick, urecv[:, HD:SLOT, :].astype(F32), 0.0), axis=1)
    state = jnp.zeros((HD, HD), F32)
    run = jnp.zeros((1, HD), F32)
    for j in range(NZ):
        lst[j] = state
        lead[j:j + 1] = run
        state = state * jnp.exp(logs[j:j + 1]) + urecv[j, 0:HD].astype(F32)
        run = run + logs[j:j + 1]
    rst[0:HD] = state.astype(BF)
    rst[HD:SLOT] = two_terms(run + jnp.zeros((HEADS, HD), F32))

    def row_copy(i):
        return remote(rst, rrecv.at[y], row_s.at[i - 1], row_r.at[y], at(i, 0))

    for i in range(1, NY):
        row_copy(i).start()
    z_forward(0)
    z_forward(2)
    for i in range(1, NY):
        ys = lax.rem(y + i, NY)
        remote(rst, rrecv.at[ys], row_s.at[0], row_r.at[ys], at(0, 0)).wait_recv()
    state = jnp.zeros((HD, HD), F32)
    for j in range(NY - 1):
        logs = rrecv[j, HD:HD + 1].astype(F32) + rrecv[j, HD + HEADS:HD + HEADS + 1].astype(F32)
        state = jnp.where(j < y, state * jnp.exp(logs) + rrecv[j, 0:HD].astype(F32), state)
    for j in range(NZ):
        pst[j] = (lst[j] + jnp.exp(lead[j:j + 1]) * state).astype(BF)
    send_z(pst, precv, 1)
    precv[z] = pst[z]
    z_forward(1)
    z_forward(3)
    turn(1, (0, 2))
    sent_z(pst, precv, 1).wait_recv()

    def a_send(i):
        src = ab.at[pl.ds(i * HALF, HALF)]
        dst = ab.at[pl.ds(TOK + i * HALF, HALF)]
        return remote(src, dst, a_s.at[i], a_r.at[i], at(0, -1 if i == 0 else 1))

    for i in range(HEADS):
        cols = slice(i * HD, (i + 1) * HD)
        att = intra[:, cols] + jnp.exp(colc[:, i:i + 1]) * nn(qb[:, cols], precv[i])
        moment = jnp.mean(att * att, axis=1, keepdims=True)
        ab[0:TOK, cols] = (att * lax.rsqrt(moment + 1e-6) * gain_ref[i:i + 1, :]).astype(BF)
    a_send(0).start()
    a_send(1).start()
    turn(1, (1, 3))

    def names(unit):
        qs, r, half = unit
        yy = lax.rem(y + fold(r), NY)
        k = kq(qs[0])
        if len(qs) == 2:
            k = k // 2 * 2
        far = lax.rem(x + NX - yy, NX)
        return yy, half, pl.ds(k, len(qs)), (k // 2) == c, pl.ds(lax.rem(k, 2), len(qs)), far

    def mate_copy(n, unit):
        yy, half, ks, mine, kk, far = names(unit)
        ref = dbuf.at[yy, half, ks]
        return remote(ref, ref, d_s.at[n], d_r.at[n], mate)

    def relay_copy(n, unit, b):
        yy, half, ks, mine, kk, far = names(unit)
        to = along_x(lax.rem(x + (1 if b == 0 else NX - 1), NX))
        return remote(dbuf.at[yy, half, ks, cut(b)], relay.at[half, yy, ks], x_s.at[n, b], r_r.at[n], to)

    def x_copy(n, unit, g, b):
        yy, half, ks, mine, kk, far = names(unit)
        part = pl.ds(pl.multiple_of(b * CUT, CUT), CUT)
        src = dbuf.at[yy, half, ks, part]
        dst = xrecv.at[g, half, kk, part]
        return remote(src, dst, x_s.at[n, b], x_r.at[n, g, b], along_x(yy))

    def compute(n, unit):
        yy, half, ks, mine, kk, far = names(unit)
        m = len(unit[0])
        res = nt(wb[yy, ks].reshape(m * PIECE, WIDTH), ab[half * TOK:(half + 1) * TOK]).reshape(m, PIECE, TOK)

        @pl.when(mine)
        def _():
            fbuf[n % 4, 0:m] = res

        @pl.when(jnp.logical_not(mine))
        def _():
            dbuf[yy, half, ks] = res.astype(BF)
            mate_copy(n, unit).start()

    def pair(n, unit):
        yy, half, ks, mine, kk, far = names(unit)
        m = len(unit[0])

        @pl.when(mine)
        def _():
            mate_copy(n, unit).wait_recv()
            val = (fbuf[n % 4, 0:m] + dbuf[yy, half, ks].astype(F32)).astype(BF)

            @pl.when(far == 0)
            def _():
                own[half, kk] = val

            @pl.when(far != 0)
            def _():
                dbuf[yy, half, ks] = val

            @pl.when(far == 2)
            def _():
                relay_copy(n, unit, 0).start()
                relay_copy(n, unit, 1).start()

            @pl.when(far == 1)
            def _():
                x_copy(n, unit, 1, 0).start()

            @pl.when(far == 3)
            def _():
                x_copy(n, unit, 0, 1).start()

    def passed(n, unit):
        yy, half, ks, mine, kk, far = names(unit)

        @pl.when(jnp.logical_and(mine, lax.rem(far, 2) == 1))
        def _():
            g = 1 - far // 2
            part = pl.ds(pl.multiple_of(g * CUT, CUT), CUT)
            came = relay.at[half, yy, ks]
            remote(came, came, x_s.at[n, 0], r_r.at[n], mate).wait_recv()
            dbuf[yy, half, ks, part] = (dbuf[yy, half, ks, part].astype(F32) + came[...].astype(F32)).astype(BF)
            x_copy(n, unit, g, g).start()

    def back(kk, i):
        src = fin.at[kk, :, pl.ds(i * HALF, HALF)]
        dst = otb.at[2 * kk + h, :, pl.ds(i * HALF, HALF)]
        return remote(src, dst, b_s.at[kk, i], b_r.at[kk, i], at(0, 1 if i == 0 else -1))

    def back_wait(kk, i):
        ref = otb.at[2 * kk + 1 - h, :, pl.ds(i * HALF, HALF)]
        remote(ref, ref, b_s.at[kk, i], b_r.at[kk, i], at(0, 0)).wait_recv()

    def total(n, unit):
        yy, half, ks, mine, kk, far = names(unit)
        m = len(unit[0])

        @pl.when(jnp.logical_and(mine, far == 0))
        def _():
            for g in range(2):
                for b in range(2):
                    ref = xrecv.at[g, half, kk, cut(b)]
                    remote(ref, ref, x_s.at[n, 0], x_r.at[n, g, b], mate).wait_recv()
            for j in range(m):
                one = j if m == 2 else lax.rem(kq(unit[0][0]), 2)
                acc = xrecv[0, half, one].astype(F32) + xrecv[1, half, one].astype(F32)
                acc = (acc + own[half, one].astype(F32)).astype(BF)
                if half == 0:
                    otb[2 * one + h] = acc
                else:
                    fin[one] = acc
                    back(one, 0).start()
                    back(one, 1).start()

    order = []
    hooks = {}

    def add(qs, rows, halves):
        for r in rows:
            order.extend([(qs, r, half) for half in halves])

    def hook(fn):
        hooks.setdefault(len(order), []).append(fn)

    def a_wait():
        for i in range(2):
            a_send(i).wait_recv()

    add((0,), (0, 1, 2), (0,))
    hook(lambda: y_last(0))
    add((0,), (3,), (0,))
    add((1,), (0, 1, 2), (0,))
    hook(lambda: turn(2, (0, 2)))
    hook(lambda: y_last(1))
    add((1,), (3,), (0,))
    hook(lambda: turn(2, (1, 3)))
    add((2,), (0, 1, 2), (0,))
    hook(a_wait)
    add((0, 1), (0, 1), (1,))
    hook(lambda: turn(3, (0, 2)))
    add((0, 1), (2, 3), (1,))
    add((2,), (0, 1, 2), (1,))
    hook(lambda: y_last(2))
    add((2,), (3,), (1, 0))
    add((3,), (0,), (1, 0))
    hook(lambda: turn(3, (1, 3)))
    add((3,), (1, 2), (1, 0))
    hook(lambda: y_last(3))
    add((3,), (3,), (1, 0))

    stages = ((0, compute), (3, pair), (9, passed), (20, total))
    for n in range(len(order) + stages[-1][0]):
        for fn in hooks.get(n, ()):
            fn()
        for lag, fn in stages:
            if 0 <= n - lag < len(order):
                fn(n - lag, order[n - lag])

    for kk in range(2):
        for i in range(2):
            back_wait(kk, i)
    final = pltpu.make_async_copy(otb, out_hbm, out_sem.at[0])
    final.start()

    for b in CHUNKS:
        for i in range(3):
            wz(b, i).wait_send()
            for q in range(4):
                wy(q, b, i).wait_send()
    for i in range(2):
        a_send(i).wait_send()
    sent_z(ust, urecv, 0).wait_send()
    sent_z(pst, precv, 1).wait_send()
    for i in range(1, NY):
        row_copy(i).wait_send()
    for n, unit in enumerate(order):
        yy, half, ks, mine, kk, far = names(unit)

        @pl.when(jnp.logical_and(mine, far != 0))
        def _():
            relay_copy(n, unit, 0).wait_send()
            relay_copy(n, unit, 1).wait_send()

        @pl.when(jnp.logical_not(mine))
        def _():
            mate_copy(n, unit).wait_send()

        @pl.when(jnp.logical_and(jnp.logical_and(mine, far == 0), half == 1))
        def _():
            for j in range(len(unit[0])):
                one = j if len(unit[0]) == 2 else lax.rem(kq(unit[0][0]), 2)
                back(one, 0).wait_send()
                back(one, 1).wait_send()

    final.wait()


def shards(query_rows, key_rows, value_rows, log_decay, norm_gain, out_proj):
    vmem = pltpu.VMEM
    dma = pltpu.SemaphoreType.DMA
    anywhere = pl.BlockSpec(memory_space=pl.ANY)
    near = pl.BlockSpec(memory_space=pltpu.VMEM)
    out = pl.pallas_call(
        kernel,
        name="parity_attention",
        out_shape=jax.ShapeDtypeStruct((4, PIECE, TOK), BF),
        in_specs=[anywhere] * 4 + [near] * 2,
        out_specs=anywhere,
        scratch_shapes=[
            vmem((TOK, WIDTH), BF),
            vmem((TOK, WIDTH), BF),
            vmem((TOK, WIDTH), BF),
            vmem((NY, 4, PIECE, WIDTH), BF),
            vmem((2 * TOK, WIDTH), BF),
            vmem((TOK, WIDTH), F32),
            vmem((TOK, HD), F32),
            vmem((HEADS, TOK), F32),
            vmem((NZ, SLOT, HD), BF),
            vmem((NZ, SLOT, HD), BF),
            vmem((NZ, HD, HD), F32),
            vmem((NZ, HD), F32),
            vmem((SLOT, HD), BF),
            vmem((NY, SLOT, HD), BF),
            vmem((NZ, HD, HD), BF),
            vmem((NZ, HD, HD), BF),
            vmem((NY, 2, 4, PIECE, TOK), BF),
            vmem((4, 2, PIECE, TOK), F32),
            vmem((2, NY, 4, CUT, TOK), BF),
            vmem((2, 2, PIECE, TOK), BF),
            vmem((2, 2, 2, PIECE, TOK), BF),
            vmem((2, PIECE, TOK), BF),
            vmem((4, PIECE, TOK), BF),
            dma((4,)),
            dma((1,)),
            dma((4, 3)),
            dma((4, 3)),
            dma((4, 4, 3)),
            dma((4, 4, 3)),
            dma((2,)),
            dma((2,)),
            dma((NY - 1,)),
            dma((NY,)),
            dma((2,)),
            dma((2,)),
            dma((32,)),
            dma((32,)),
            dma((32, 2)),
            dma((32, 2, 2)),
            dma((32,)),
            dma((2, 2)),
            dma((2, 2)),
        ],
        compiler_params=pltpu.CompilerParams(
            collective_id=0, has_side_effects=True, vmem_limit_bytes=56 * 2**20
        ),
        cost_estimate=pl.CostEstimate(flops=8 * 10**9, bytes_accessed=5 * 2**20, transcendentals=2 * 10**6),
    )(query_rows, key_rows, value_rows, out_proj.T, log_decay.T, norm_gain.reshape(HEADS, HD))
    return out.reshape(4 * PIECE, TOK).T


def solution(mesh):
    return jax.shard_map(
        shards,
        mesh=mesh,
        in_specs=(
            P("section", "group"),
            P("section", "group"),
            P("section", "group"),
            P("section", "group"),
            P("group"),
            P("group", "section"),
        ),
        out_specs=P("section", "group"),
        check_vma=False,
    )
```

```python
import functools

import jax
import jax.numpy as jnp
from jax import lax
from jax.experimental import pallas as pl
from jax.experimental.pallas import tpu as pltpu
from jax.sharding import PartitionSpec as P

BF = jnp.bfloat16
F32 = jnp.float32
MESH = pl.DeviceIdType.MESH
TOK = 512
HALF = 256
HEADS = 8
HD = 128
WIDTH = HEADS * HD
PIECE = 192
CUT = 96
CHUNK = 48
CHUNKS = (0, 2, 1, 3)
NY, NZ, NX = 4, 8, 4
SLOT = HD + 16


def nt(a, b):
    return lax.dot_general(a, b, (((1,), (1,)), ((), ())), preferred_element_type=F32)


def tn(a, b):
    return lax.dot_general(a, b, (((0,), (0,)), ((), ())), preferred_element_type=F32)


def nn(a, b):
    return jnp.dot(a, b, preferred_element_type=F32)


EARLY = {7: (1, 3)}
LAGS = (3, 9, 20)


def fold(i):
    return i + i // 2 - 2 * (i // 3)


def kernel(
    q_hbm, k_hbm, v_hbm, w_hbm, decay_ref, gain_ref, out_hbm,
    qb, kb, vb, wb, ab, intra, colc, rowc, ust, urecv, lst, lead, rst, rrecv, pst, precv,
    dbuf, fbuf, relay, own, xrecv, fin, otb,
    load_sem, out_sem, wz_s, wz_r, wy_s, wy_r, st_s, st_r, row_s, row_r, a_s, a_r, d_s, d_r, x_s, x_r, r_r, b_s, b_r,
):
    sec = lax.axis_index("section")
    grp = lax.axis_index("group")
    y, z = sec // NZ, lax.rem(sec, NZ)
    x, c = grp // 2, lax.rem(grp, 2)
    h, k0 = lax.rem(z, 2), z // 2

    def at(dy, dz):
        return (lax.rem(y + dy + NY, NY) * NZ + lax.rem(z + dz + NZ, NZ), grp)

    mate = (sec, x * 2 + 1 - c)

    def along_x(xx):
        return (sec, xx * 2 + c)

    def remote(src, dst, ssem, rsem, dev):
        return pltpu.make_async_remote_copy(
            src_ref=src, dst_ref=dst, send_sem=ssem, recv_sem=rsem, device_id=dev, device_id_type=MESH
        )

    loads = [
        pltpu.make_async_copy(s, d, load_sem.at[i])
        for i, (s, d) in enumerate(((w_hbm, wb.at[y, k0]), (k_hbm, kb), (v_hbm, vb), (q_hbm, qb)))
    ]
    for cp in loads:
        cp.start()
    bar = pltpu.get_barrier_semaphore()
    peers = [at(0, i) for i in range(1, NZ)] + [at(i, 0) for i in range(1, NY)]
    peers += [along_x(lax.rem(x + i, NX)) for i in (1, 3)] + [mate]
    for dev in peers:
        pl.semaphore_signal(bar, inc=1, device_id=dev, device_id_type=MESH)

    d = decay_ref[...]
    hi = d.astype(BF).astype(F32)
    mid = (d - hi).astype(BF).astype(F32)
    low = d - hi - mid
    tri = (
        lax.broadcasted_iota(jnp.int32, (TOK, TOK), 0) <= lax.broadcasted_iota(jnp.int32, (TOK, TOK), 1)
    ).astype(F32).astype(BF)
    cum = nn(jnp.concatenate([hi, mid, low, jnp.zeros_like(d)], axis=0).astype(BF), tri)
    cum = cum[0:HEADS] + (cum[HEADS:2 * HEADS] + cum[2 * HEADS:3 * HEADS])
    rowc[...] = cum
    colc[...] = jnp.concatenate([cum, jnp.zeros((HD - HEADS, TOK), F32)], axis=0).T

    def two_terms(val):
        top = val.astype(BF).astype(F32)
        return jnp.concatenate([top, val - top], axis=0).astype(BF)

    loads[0].wait()
    pl.semaphore_wait(bar, len(peers))

    def cut(b):
        return pl.ds(b * CUT, CUT)

    def chunk(b):
        return pl.ds(b * CHUNK, CHUNK)

    def kq(q):
        turn = 1 + 2 * lax.rem(k0, 2)
        return lax.rem(k0 + (0, turn, 4 - turn, 2)[q], 4)

    def wz(b, i):
        if i < 2:
            ref = wb.at[y, k0, chunk(b)]
            dz = 2 if i == 0 else -2
        else:
            ref = wb.at[y, lax.rem(k0 + (3 if b < 2 else 1), 4), chunk(b)]
            dz = 2 if b < 2 else -2
        return remote(ref, ref, wz_s.at[b, i], wz_r.at[b, i], at(0, dz))

    def wz_wait(b, i):
        ref = wb.at[y, lax.rem(k0 + (3, 1, 2)[i], 4), chunk(b)]
        remote(ref, ref, wz_s.at[b, i], wz_r.at[b, i], at(0, 0)).wait_recv()

    def wy(q, b, i):
        if i < 2:
            ref = wb.at[y, kq(q), chunk(b)]
            dy = 1 if i == 0 else -1
        else:
            ref = wb.at[lax.rem(y + (3 if b < 2 else 1), NY), kq(q), chunk(b)]
            dy = 1 if b < 2 else -1
        return remote(ref, ref, wy_s.at[q, b, i], wy_r.at[q, b, i], at(dy, 0))

    def wy_wait(q, b, i):
        ref = wb.at[lax.rem(y + (3, 1, 2)[i], NY), kq(q), chunk(b)]
        remote(ref, ref, wy_s.at[q, b, i], wy_r.at[q, b, i], at(0, 0)).wait_recv()

    def y_send(q, b):
        wy(q, b, 0).start()
        wy(q, b, 1).start()

    def y_forward(q, b):
        wy_wait(q, b, b // 2)
        wy(q, b, 2).start()
        wy_wait(q, b, 1 - b // 2)

    def turn(q, bs):
        for b in bs:
            y_forward(q, b)
            if q < 3:
                if q == 2:
                    wz_wait(b, 2)
                y_send(q + 1, b)

    def y_last(q):
        for b in CHUNKS:
            wy_wait(q, b, 2)

    def z_forward(b):
        wz_wait(b, b // 2)
        wz(b, 2).start()
        wz_wait(b, 1 - b // 2)
        y_send(1, b)

    for b in CHUNKS:
        y_send(0, b)
    for b in (0, 2):
        wz(b, 0).start()
        wz(b, 1).start()

    loads[1].wait()
    loads[2].wait()
    tail = two_terms(cum[:, TOK - 1:TOK] + jnp.zeros((HEADS, HD), F32))
    for i in range(HEADS):
        col = colc[:, i:i + 1]
        last = colc[TOK - 1:TOK, i:i + 1]
        keys = (kb[:, i * HD:(i + 1) * HD].astype(F32) * jnp.exp(last - col)).astype(BF)
        ust[i, 0:HD] = tn(keys, vb[:, i * HD:(i + 1) * HD]).astype(BF)
        ust[i, HD:SLOT] = tail
    def send_z(src, dst, i):
        def one(o, _):
            to = lax.rem(z + o, NZ)
            remote(src.at[to], dst.at[z], st_s.at[i], st_r.at[i], (y * NZ + to, grp)).start()
            return 0

        lax.fori_loop(1, NZ, one, 0)

    def sent_z(src, dst, i):
        some = pl.ds(0, NZ - 1)
        return remote(src.at[some], dst.at[some], st_s.at[i], st_r.at[i], at(0, 0))

    send_z(ust, urecv, 0)

    loads[3].wait()
    causal = lax.broadcasted_iota(jnp.int32, (HALF, HALF), 0) >= lax.broadcasted_iota(jnp.int32, (HALF, HALF), 1)

    def inside(i):
        cols = slice(i * HD, (i + 1) * HD)
        for b in range(2):
            rows = slice(b * HALF, (b + 1) * HALF)
            qt = qb[rows, cols]
            col = colc[rows, i:i + 1]
            acc = None
            for e in range(b + 1):
                sl = slice(e * HALF, (e + 1) * HALF)
                scores = nt(qt, kb[sl, cols])
                spread = col - rowc[i:i + 1, sl]
                if e == b:
                    spread = jnp.where(causal, spread, -1e30)
                weights = (scores * jnp.exp(spread)).astype(BF)
                term = nn(weights, vb[sl, cols])
                acc = term if acc is None else acc + term
            intra[rows, cols] = acc

    for i in range(HEADS):
        inside(i)
        if i in EARLY:
            for b in EARLY[i]:
                wz(b, 0).start()
                wz(b, 1).start()

    urecv[z] = ust[z]
    for b in CHUNKS:
        y_forward(0, b)
    sent_z(ust, urecv, 0).wait_recv()
    pick = lax.rem(lax.broadcasted_iota(jnp.int32, (NZ, SLOT - HD, HD), 1), HEADS) == z
    logs = jnp.sum(jnp.where(pick, urecv[:, HD:SLOT, :].astype(F32), 0.0), axis=1)
    state = jnp.zeros((HD, HD), F32)
    run = jnp.zeros((1, HD), F32)
    for j in range(NZ):
        lst[j] = state
        lead[j:j + 1] = run
        state = state * jnp.exp(logs[j:j + 1]) + urecv[j, 0:HD].astype(F32)
        run = run + logs[j:j + 1]
    rst[0:HD] = state.astype(BF)
    rst[HD:SLOT] = two_terms(run + jnp.zeros((HEADS, HD), F32))

    def row_copy(i):
        return remote(rst, rrecv.at[y], row_s.at[i - 1], row_r.at[y], at(i, 0))

    for i in range(1, NY):
        row_copy(i).start()
    z_forward(0)
    z_forward(2)
    for i in range(1, NY):
        ys = lax.rem(y + i, NY)
        remote(rst, rrecv.at[ys], row_s.at[0], row_r.at[ys], at(0, 0)).wait_recv()
    state = jnp.zeros((HD, HD), F32)
    for j in range(NY - 1):
        logs = rrecv[j, HD:HD + 1].astype(F32) + rrecv[j, HD + HEADS:HD + HEADS + 1].astype(F32)
        state = jnp.where(j < y, state * jnp.exp(logs) + rrecv[j, 0:HD].astype(F32), state)
    for j in range(NZ):
        pst[j] = (lst[j] + jnp.exp(lead[j:j + 1]) * state).astype(BF)
    send_z(pst, precv, 1)
    precv[z] = pst[z]
    z_forward(1)
    z_forward(3)
    turn(1, (0, 2))
    sent_z(pst, precv, 1).wait_recv()

    def a_send(i):
        src = ab.at[pl.ds(i * HALF, HALF)]
        dst = ab.at[pl.ds(TOK + i * HALF, HALF)]
        return remote(src, dst, a_s.at[i], a_r.at[i], at(0, -1 if i == 0 else 1))

    for i in range(HEADS):
        cols = slice(i * HD, (i + 1) * HD)
        att = intra[:, cols] + jnp.exp(colc[:, i:i + 1]) * nn(qb[:, cols], precv[i])
        moment = jnp.mean(att * att, axis=1, keepdims=True)
        ab[0:TOK, cols] = (att * lax.rsqrt(moment + 1e-6) * gain_ref[i:i + 1, :]).astype(BF)
    a_send(0).start()
    a_send(1).start()
    turn(1, (1, 3))

    def names(unit):
        qs, r, half = unit
        yy = lax.rem(y + fold(r), NY)
        k = kq(qs[0])
        if len(qs) == 2:
            k = k // 2 * 2
        far = lax.rem(x + NX - yy, NX)
        return yy, half, pl.ds(k, len(qs)), (k // 2) == c, pl.ds(lax.rem(k, 2), len(qs)), far

    def mate_copy(n, unit):
        yy, half, ks, mine, kk, far = names(unit)
        ref = dbuf.at[yy, half, ks]
        return remote(ref, ref, d_s.at[n], d_r.at[n], mate)

    def relay_copy(n, unit, b):
        yy, half, ks, mine, kk, far = names(unit)
        to = along_x(lax.rem(x + (1 if b == 0 else NX - 1), NX))
        return remote(dbuf.at[yy, half, ks, cut(b)], relay.at[half, yy, ks], x_s.at[n, b], r_r.at[n], to)

    def x_copy(n, unit, g, b):
        yy, half, ks, mine, kk, far = names(unit)
        part = pl.ds(pl.multiple_of(b * CUT, CUT), CUT)
        src = dbuf.at[yy, half, ks, part]
        dst = xrecv.at[g, half, kk, part]
        return remote(src, dst, x_s.at[n, b], x_r.at[n, g, b], along_x(yy))

    def compute(n, unit):
        yy, half, ks, mine, kk, far = names(unit)
        m = len(unit[0])
        res = nt(wb[yy, ks].reshape(m * PIECE, WIDTH), ab[half * TOK:(half + 1) * TOK]).reshape(m, PIECE, TOK)

        @pl.when(mine)
        def _():
            fbuf[n % 8, 0:m] = res

        @pl.when(jnp.logical_not(mine))
        def _():
            dbuf[yy, half, ks] = res.astype(BF)
            mate_copy(n, unit).start()

    def pair(n, unit):
        yy, half, ks, mine, kk, far = names(unit)
        m = len(unit[0])

        @pl.when(mine)
        def _():
            mate_copy(n, unit).wait_recv()
            val = (fbuf[n % 8, 0:m] + dbuf[yy, half, ks].astype(F32)).astype(BF)

            @pl.when(far == 0)
            def _():
                own[half, kk] = val

            @pl.when(far != 0)
            def _():
                dbuf[yy, half, ks] = val

            @pl.when(far == 2)
            def _():
                relay_copy(n, unit, 0).start()
                relay_copy(n, unit, 1).start()

            @pl.when(far == 1)
            def _():
                x_copy(n, unit, 1, 0).start()

            @pl.when(far == 3)
            def _():
                x_copy(n, unit, 0, 1).start()

    def passed(n, unit):
        yy, half, ks, mine, kk, far = names(unit)

        @pl.when(jnp.logical_and(mine, lax.rem(far, 2) == 1))
        def _():
            g = 1 - far // 2
            part = pl.ds(pl.multiple_of(g * CUT, CUT), CUT)
            came = relay.at[half, yy, ks]
            remote(came, came, x_s.at[n, 0], r_r.at[n], mate).wait_recv()
            dbuf[yy, half, ks, part] = (dbuf[yy, half, ks, part].astype(F32) + came[...].astype(F32)).astype(BF)
            x_copy(n, unit, g, g).start()

    def back(kk, i):
        src = fin.at[kk, :, pl.ds(i * HALF, HALF)]
        dst = otb.at[2 * kk + h, :, pl.ds(i * HALF, HALF)]
        return remote(src, dst, b_s.at[kk, i], b_r.at[kk, i], at(0, 1 if i == 0 else -1))

    def back_wait(kk, i):
        ref = otb.at[2 * kk + 1 - h, :, pl.ds(i * HALF, HALF)]
        remote(ref, ref, b_s.at[kk, i], b_r.at[kk, i], at(0, 0)).wait_recv()

    def total(n, unit):
        yy, half, ks, mine, kk, far = names(unit)
        m = len(unit[0])

        @pl.when(jnp.logical_and(mine, far == 0))
        def _():
            for g in range(2):
                for b in range(2):
                    ref = xrecv.at[g, half, kk, cut(b)]
                    remote(ref, ref, x_s.at[n, 0], x_r.at[n, g, b], mate).wait_recv()
            for j in range(m):
                one = j if m == 2 else lax.rem(kq(unit[0][0]), 2)
                acc = xrecv[0, half, one].astype(F32) + xrecv[1, half, one].astype(F32)
                acc = (acc + own[half, one].astype(F32)).astype(BF)
                if half == 0:
                    otb[2 * one + h] = acc
                else:
                    fin[one] = acc
                    back(one, 0).start()
                    back(one, 1).start()

    order = []
    hooks = {}

    def add(qs, rows, halves):
        for r in rows:
            order.extend([(qs, r, half) for half in halves])

    def hook(fn):
        hooks.setdefault(len(order), []).append(fn)

    def a_wait():
        for i in range(2):
            a_send(i).wait_recv()

    add((0,), (0, 1, 2), (0,))
    hook(lambda: y_last(0))
    add((0,), (3,), (0,))
    add((1,), (0, 1, 2), (0,))
    hook(lambda: turn(2, (0, 2)))
    hook(lambda: y_last(1))
    add((1,), (3,), (0,))
    hook(lambda: turn(2, (1, 3)))
    add((2,), (0, 1, 2), (0,))
    hook(a_wait)
    add((0, 1), (0, 1), (1,))
    hook(lambda: turn(3, (0, 2)))
    add((0, 1), (2, 3), (1,))
    add((2,), (0, 1, 2), (1,))
    hook(lambda: y_last(2))
    add((2,), (3,), (1, 0))
    add((3,), (0,), (1, 0))
    hook(lambda: turn(3, (1, 3)))
    add((3,), (1, 2), (1, 0))
    hook(lambda: y_last(3))
    add((3,), (3,), (1, 0))

    stages = ((0, compute), (LAGS[0], pair), (LAGS[1], passed), (LAGS[2], total))
    for n in range(len(order) + stages[-1][0]):
        for fn in hooks.get(n, ()):
            fn()
        for lag, fn in stages:
            if 0 <= n - lag < len(order):
                fn(n - lag, order[n - lag])

    def out_copy(i):
        return pltpu.make_async_copy(otb.at[i], out_hbm.at[i], out_sem.at[i])

    for kk in range(2):
        out_copy(2 * kk + h).start()
    for kk in range(2):
        for i in range(2):
            back_wait(kk, i)
        out_copy(2 * kk + 1 - h).start()

    for b in CHUNKS:
        for i in range(3):
            wz(b, i).wait_send()
            for q in range(4):
                wy(q, b, i).wait_send()
    for i in range(2):
        a_send(i).wait_send()
    sent_z(ust, urecv, 0).wait_send()
    sent_z(pst, precv, 1).wait_send()
    for i in range(1, NY):
        row_copy(i).wait_send()
    for n, unit in enumerate(order):
        yy, half, ks, mine, kk, far = names(unit)

        @pl.when(jnp.logical_and(mine, far != 0))
        def _():
            relay_copy(n, unit, 0).wait_send()
            relay_copy(n, unit, 1).wait_send()

        @pl.when(jnp.logical_not(mine))
        def _():
            mate_copy(n, unit).wait_send()

        @pl.when(jnp.logical_and(jnp.logical_and(mine, far == 0), half == 1))
        def _():
            for j in range(len(unit[0])):
                one = j if len(unit[0]) == 2 else lax.rem(kq(unit[0][0]), 2)
                back(one, 0).wait_send()
                back(one, 1).wait_send()

    for i in range(4):
        out_copy(i).wait()


def shards(query_rows, key_rows, value_rows, log_decay, norm_gain, out_proj):
    vmem = pltpu.VMEM
    dma = pltpu.SemaphoreType.DMA
    anywhere = pl.BlockSpec(memory_space=pl.ANY)
    near = pl.BlockSpec(memory_space=pltpu.VMEM)
    out = pl.pallas_call(
        kernel,
        name="parity_attention",
        out_shape=jax.ShapeDtypeStruct((4, PIECE, TOK), BF),
        in_specs=[anywhere] * 4 + [near] * 2,
        out_specs=anywhere,
        scratch_shapes=[
            vmem((TOK, WIDTH), BF),
            vmem((TOK, WIDTH), BF),
            vmem((TOK, WIDTH), BF),
            vmem((NY, 4, PIECE, WIDTH), BF),
            vmem((2 * TOK, WIDTH), BF),
            vmem((TOK, WIDTH), F32),
            vmem((TOK, HD), F32),
            vmem((HEADS, TOK), F32),
            vmem((NZ, SLOT, HD), BF),
            vmem((NZ, SLOT, HD), BF),
            vmem((NZ, HD, HD), F32),
            vmem((NZ, HD), F32),
            vmem((SLOT, HD), BF),
            vmem((NY, SLOT, HD), BF),
            vmem((NZ, HD, HD), BF),
            vmem((NZ, HD, HD), BF),
            vmem((NY, 2, 4, PIECE, TOK), BF),
            vmem((8, 2, PIECE, TOK), F32),
            vmem((2, NY, 4, CUT, TOK), BF),
            vmem((2, 2, PIECE, TOK), BF),
            vmem((2, 2, 2, PIECE, TOK), BF),
            vmem((2, PIECE, TOK), BF),
            vmem((4, PIECE, TOK), BF),
            dma((4,)),
            dma((4,)),
            dma((4, 3)),
            dma((4, 3)),
            dma((4, 4, 3)),
            dma((4, 4, 3)),
            dma((2,)),
            dma((2,)),
            dma((NY - 1,)),
            dma((NY,)),
            dma((2,)),
            dma((2,)),
            dma((32,)),
            dma((32,)),
            dma((32, 2)),
            dma((32, 2, 2)),
            dma((32,)),
            dma((2, 2)),
            dma((2, 2)),
        ],
        compiler_params=pltpu.CompilerParams(
            collective_id=0, has_side_effects=True, vmem_limit_bytes=56 * 2**20
        ),
        cost_estimate=pl.CostEstimate(flops=8 * 10**9, bytes_accessed=5 * 2**20, transcendentals=2 * 10**6),
    )(query_rows, key_rows, value_rows, out_proj.T, log_decay.T, norm_gain.reshape(HEADS, HD))
    return out.reshape(4 * PIECE, TOK).T


def solution(mesh):
    return jax.shard_map(
        shards,
        mesh=mesh,
        in_specs=(
            P("section", "group"),
            P("section", "group"),
            P("section", "group"),
            P("section", "group"),
            P("group"),
            P("group", "section"),
        ),
        out_specs=P("section", "group"),
        check_vma=False,
    )
```

```python
import functools

import jax
import jax.numpy as jnp
from jax import lax
from jax.experimental import pallas as pl
from jax.experimental.pallas import tpu as pltpu
from jax.sharding import PartitionSpec as P

BF = jnp.bfloat16
F32 = jnp.float32
MESH = pl.DeviceIdType.MESH
TOK = 512
HALF = 256
HEADS = 8
HD = 128
WIDTH = HEADS * HD
PIECE = 192
CUT = 96
CHUNK = 48
CHUNKS = (0, 2, 1, 3)
NY, NZ, NX = 4, 8, 4
SLOT = HD + 16


def nt(a, b):
    return lax.dot_general(a, b, (((1,), (1,)), ((), ())), preferred_element_type=F32)


def tn(a, b):
    return lax.dot_general(a, b, (((0,), (0,)), ((), ())), preferred_element_type=F32)


def nn(a, b):
    return jnp.dot(a, b, preferred_element_type=F32)


EARLY = {7: (1, 3)}
LAGS = (2, 7, 14)


def fold(i):
    return i + i // 2 - 2 * (i // 3)


def kernel(
    q_hbm, k_hbm, v_hbm, w_hbm, decay_ref, gain_ref, out_hbm,
    qb, kb, vb, wb, ab, intra, colc, rowc, ust, urecv, lst, lead, rst, rrecv, pst, precv,
    dbuf, fbuf, relay, own, xrecv, fin, otb,
    load_sem, out_sem, wz_s, wz_r, wy_s, wy_r, st_s, st_r, row_s, row_r, a_s, a_r, d_s, d_r, x_s, x_r, r_r, b_s, b_r,
):
    sec = lax.axis_index("section")
    grp = lax.axis_index("group")
    y, z = sec // NZ, lax.rem(sec, NZ)
    x, c = grp // 2, lax.rem(grp, 2)
    h, k0 = lax.rem(z, 2), z // 2

    def at(dy, dz):
        return (lax.rem(y + dy + NY, NY) * NZ + lax.rem(z + dz + NZ, NZ), grp)

    mate = (sec, x * 2 + 1 - c)

    def along_x(xx):
        return (sec, xx * 2 + c)

    def remote(src, dst, ssem, rsem, dev):
        return pltpu.make_async_remote_copy(
            src_ref=src, dst_ref=dst, send_sem=ssem, recv_sem=rsem, device_id=dev, device_id_type=MESH
        )

    loads = [
        pltpu.make_async_copy(s, d, load_sem.at[i])
        for i, (s, d) in enumerate(((w_hbm, wb.at[y, k0]), (k_hbm, kb), (v_hbm, vb), (q_hbm, qb)))
    ]
    for cp in loads:
        cp.start()
    bar = pltpu.get_barrier_semaphore()
    peers = [at(0, i) for i in range(1, NZ)] + [at(i, 0) for i in range(1, NY)]
    peers += [along_x(lax.rem(x + i, NX)) for i in (1, 3)] + [mate]
    for dev in peers:
        pl.semaphore_signal(bar, inc=1, device_id=dev, device_id_type=MESH)

    loads[0].wait()
    pl.semaphore_wait(bar, len(peers))

    def cut(b):
        return pl.ds(b * CUT, CUT)

    def chunk(b):
        return pl.ds(b * CHUNK, CHUNK)

    def kq(q):
        turn = 1 + 2 * lax.rem(k0, 2)
        return lax.rem(k0 + (0, turn, 4 - turn, 2)[q], 4)

    def wz(b, i):
        if i < 2:
            ref = wb.at[y, k0, chunk(b)]
            dz = 2 if i == 0 else -2
        else:
            ref = wb.at[y, lax.rem(k0 + (3 if b < 2 else 1), 4), chunk(b)]
            dz = 2 if b < 2 else -2
        return remote(ref, ref, wz_s.at[b, i], wz_r.at[b, i], at(0, dz))

    def wz_wait(b, i):
        ref = wb.at[y, lax.rem(k0 + (3, 1, 2)[i], 4), chunk(b)]
        remote(ref, ref, wz_s.at[b, i], wz_r.at[b, i], at(0, 0)).wait_recv()

    def wy(q, b, i):
        if i < 2:
            ref = wb.at[y, kq(q), chunk(b)]
            dy = 1 if i == 0 else -1
        else:
            ref = wb.at[lax.rem(y + (3 if b < 2 else 1), NY), kq(q), chunk(b)]
            dy = 1 if b < 2 else -1
        return remote(ref, ref, wy_s.at[q, b, i], wy_r.at[q, b, i], at(dy, 0))

    def wy_wait(q, b, i):
        ref = wb.at[lax.rem(y + (3, 1, 2)[i], NY), kq(q), chunk(b)]
        remote(ref, ref, wy_s.at[q, b, i], wy_r.at[q, b, i], at(0, 0)).wait_recv()

    def y_send(q, b):
        wy(q, b, 0).start()
        wy(q, b, 1).start()

    def y_forward(q, b):
        wy_wait(q, b, b // 2)
        wy(q, b, 2).start()
        wy_wait(q, b, 1 - b // 2)

    def turn(q, bs):
        for b in bs:
            y_forward(q, b)
            if q < 3:
                if q == 2:
                    wz_wait(b, 2)
                y_send(q + 1, b)

    def y_last(q):
        for b in CHUNKS:
            wy_wait(q, b, 2)

    def z_forward(b):
        wz_wait(b, b // 2)
        wz(b, 2).start()
        wz_wait(b, 1 - b // 2)
        y_send(1, b)

    for b in CHUNKS:
        y_send(0, b)
    for b in (0, 2):
        wz(b, 0).start()
        wz(b, 1).start()

    d = decay_ref[...]
    hi = d.astype(BF).astype(F32)
    mid = (d - hi).astype(BF).astype(F32)
    low = d - hi - mid
    tri = (
        lax.broadcasted_iota(jnp.int32, (TOK, TOK), 0) <= lax.broadcasted_iota(jnp.int32, (TOK, TOK), 1)
    ).astype(F32).astype(BF)
    cum = nn(jnp.concatenate([hi, mid, low, jnp.zeros_like(d)], axis=0).astype(BF), tri)
    cum = cum[0:HEADS] + (cum[HEADS:2 * HEADS] + cum[2 * HEADS:3 * HEADS])
    rowc[...] = cum
    colc[...] = jnp.concatenate([cum, jnp.zeros((HD - HEADS, TOK), F32)], axis=0).T

    def two_terms(val):
        top = val.astype(BF).astype(F32)
        return jnp.concatenate([top, val - top], axis=0).astype(BF)

    loads[1].wait()
    loads[2].wait()
    tail = two_terms(cum[:, TOK - 1:TOK] + jnp.zeros((HEADS, HD), F32))
    for i in range(HEADS):
        col = colc[:, i:i + 1]
        last = colc[TOK - 1:TOK, i:i + 1]
        keys = (kb[:, i * HD:(i + 1) * HD].astype(F32) * jnp.exp(last - col)).astype(BF)
        ust[i, 0:HD] = tn(keys, vb[:, i * HD:(i + 1) * HD]).astype(BF)
        ust[i, HD:SLOT] = tail
    def send_z(src, dst, i):
        def one(o, _):
            to = lax.rem(z + o, NZ)
            remote(src.at[to], dst.at[z], st_s.at[i], st_r.at[i], (y * NZ + to, grp)).start()
            return 0

        lax.fori_loop(1, NZ, one, 0)

    def sent_z(src, dst, i):
        some = pl.ds(0, NZ - 1)
        return remote(src.at[some], dst.at[some], st_s.at[i], st_r.at[i], at(0, 0))

    send_z(ust, urecv, 0)

    loads[3].wait()
    causal = lax.broadcasted_iota(jnp.int32, (HALF, HALF), 0) >= lax.broadcasted_iota(jnp.int32, (HALF, HALF), 1)

    def inside(i):
        cols = slice(i * HD, (i + 1) * HD)
        for b in range(2):
            rows = slice(b * HALF, (b + 1) * HALF)
            qt = qb[rows, cols]
            col = colc[rows, i:i + 1]
            acc = None
            for e in range(b + 1):
                sl = slice(e * HALF, (e + 1) * HALF)
                scores = nt(qt, kb[sl, cols])
                spread = col - rowc[i:i + 1, sl]
                if e == b:
                    spread = jnp.where(causal, spread, -1e30)
                weights = (scores * jnp.exp(spread)).astype(BF)
                term = nn(weights, vb[sl, cols])
                acc = term if acc is None else acc + term
            intra[rows, cols] = acc

    for i in range(HEADS):
        inside(i)
        if i in EARLY:
            for b in EARLY[i]:
                wz(b, 0).start()
                wz(b, 1).start()

    urecv[z] = ust[z]
    for b in CHUNKS:
        y_forward(0, b)
    sent_z(ust, urecv, 0).wait_recv()
    pick = lax.rem(lax.broadcasted_iota(jnp.int32, (NZ, SLOT - HD, HD), 1), HEADS) == z
    logs = jnp.sum(jnp.where(pick, urecv[:, HD:SLOT, :].astype(F32), 0.0), axis=1)
    state = jnp.zeros((HD, HD), F32)
    run = jnp.zeros((1, HD), F32)
    for j in range(NZ):
        lst[j] = state
        lead[j:j + 1] = run
        state = state * jnp.exp(logs[j:j + 1]) + urecv[j, 0:HD].astype(F32)
        run = run + logs[j:j + 1]
    rst[0:HD] = state.astype(BF)
    rst[HD:SLOT] = two_terms(run + jnp.zeros((HEADS, HD), F32))

    def row_copy(i):
        return remote(rst, rrecv.at[y], row_s.at[i - 1], row_r.at[y], at(i, 0))

    for i in range(1, NY):
        row_copy(i).start()
    z_forward(0)
    z_forward(2)
    for i in range(1, NY):
        ys = lax.rem(y + i, NY)
        remote(rst, rrecv.at[ys], row_s.at[0], row_r.at[ys], at(0, 0)).wait_recv()
    state = jnp.zeros((HD, HD), F32)
    for j in range(NY - 1):
        logs = rrecv[j, HD:HD + 1].astype(F32) + rrecv[j, HD + HEADS:HD + HEADS + 1].astype(F32)
        state = jnp.where(j < y, state * jnp.exp(logs) + rrecv[j, 0:HD].astype(F32), state)
    for j in range(NZ):
        pst[j] = (lst[j] + jnp.exp(lead[j:j + 1]) * state).astype(BF)
    send_z(pst, precv, 1)
    precv[z] = pst[z]
    z_forward(1)
    z_forward(3)
    turn(1, (0, 2))
    sent_z(pst, precv, 1).wait_recv()

    def a_send(i):
        src = ab.at[pl.ds(i * HALF, HALF)]
        dst = ab.at[pl.ds(TOK + i * HALF, HALF)]
        return remote(src, dst, a_s.at[i], a_r.at[i], at(0, -1 if i == 0 else 1))

    for i in range(HEADS):
        cols = slice(i * HD, (i + 1) * HD)
        att = intra[:, cols] + jnp.exp(colc[:, i:i + 1]) * nn(qb[:, cols], precv[i])
        moment = jnp.mean(att * att, axis=1, keepdims=True)
        ab[0:TOK, cols] = (att * lax.rsqrt(moment + 1e-6) * gain_ref[i:i + 1, :]).astype(BF)
    a_send(0).start()
    a_send(1).start()
    turn(1, (1, 3))

    def names(unit):
        qs, r, half = unit
        yy = lax.rem(y + fold(r), NY)
        k = kq(qs[0])
        if len(qs) == 2:
            k = k // 2 * 2
        far = lax.rem(x + NX - yy, NX)
        return yy, half, pl.ds(k, len(qs)), (k // 2) == c, pl.ds(lax.rem(k, 2), len(qs)), far

    def mate_copy(n, unit):
        yy, half, ks, mine, kk, far = names(unit)
        ref = dbuf.at[yy, half, ks]
        return remote(ref, ref, d_s.at[n], d_r.at[n], mate)

    def relay_copy(n, unit, b):
        yy, half, ks, mine, kk, far = names(unit)
        to = along_x(lax.rem(x + (1 if b == 0 else NX - 1), NX))
        return remote(dbuf.at[yy, half, ks, cut(b)], relay.at[half, yy, ks], x_s.at[n, b], r_r.at[n], to)

    def x_copy(n, unit, g, b):
        yy, half, ks, mine, kk, far = names(unit)
        part = pl.ds(pl.multiple_of(b * CUT, CUT), CUT)
        src = dbuf.at[yy, half, ks, part]
        dst = xrecv.at[g, half, kk, part]
        return remote(src, dst, x_s.at[n, b], x_r.at[n, g, b], along_x(yy))

    def compute(n, unit):
        yy, half, ks, mine, kk, far = names(unit)
        m = len(unit[0])
        res = nt(wb[yy, ks].reshape(m * PIECE, WIDTH), ab[half * TOK:(half + 1) * TOK]).reshape(m, PIECE, TOK)

        @pl.when(mine)
        def _():
            fbuf[n % 8, 0:m] = res

        @pl.when(jnp.logical_not(mine))
        def _():
            dbuf[yy, half, ks] = res.astype(BF)
            mate_copy(n, unit).start()

    def pair(n, unit):
        yy, half, ks, mine, kk, far = names(unit)
        m = len(unit[0])

        @pl.when(mine)
        def _():
            mate_copy(n, unit).wait_recv()
            val = (fbuf[n % 8, 0:m] + dbuf[yy, half, ks].astype(F32)).astype(BF)

            @pl.when(far == 0)
            def _():
                own[half, kk] = val

            @pl.when(far != 0)
            def _():
                dbuf[yy, half, ks] = val

            @pl.when(far == 2)
            def _():
                relay_copy(n, unit, 0).start()
                relay_copy(n, unit, 1).start()

            @pl.when(far == 1)
            def _():
                x_copy(n, unit, 1, 0).start()

            @pl.when(far == 3)
            def _():
                x_copy(n, unit, 0, 1).start()

    def passed(n, unit):
        yy, half, ks, mine, kk, far = names(unit)

        @pl.when(jnp.logical_and(mine, lax.rem(far, 2) == 1))
        def _():
            g = 1 - far // 2
            part = pl.ds(pl.multiple_of(g * CUT, CUT), CUT)
            came = relay.at[half, yy, ks]
            remote(came, came, x_s.at[n, 0], r_r.at[n], mate).wait_recv()
            dbuf[yy, half, ks, part] = (dbuf[yy, half, ks, part].astype(F32) + came[...].astype(F32)).astype(BF)
            x_copy(n, unit, g, g).start()

    def back(kk, i):
        src = fin.at[kk, :, pl.ds(i * HALF, HALF)]
        dst = otb.at[2 * kk + h, :, pl.ds(i * HALF, HALF)]
        return remote(src, dst, b_s.at[kk, i], b_r.at[kk, i], at(0, 1 if i == 0 else -1))

    def back_wait(kk, i):
        ref = otb.at[2 * kk + 1 - h, :, pl.ds(i * HALF, HALF)]
        remote(ref, ref, b_s.at[kk, i], b_r.at[kk, i], at(0, 0)).wait_recv()

    def total(n, unit):
        yy, half, ks, mine, kk, far = names(unit)
        m = len(unit[0])

        @pl.when(jnp.logical_and(mine, far == 0))
        def _():
            for g in range(2):
                for b in range(2):
                    ref = xrecv.at[g, half, kk, cut(b)]
                    remote(ref, ref, x_s.at[n, 0], x_r.at[n, g, b], mate).wait_recv()
            for j in range(m):
                one = j if m == 2 else lax.rem(kq(unit[0][0]), 2)
                acc = xrecv[0, half, one].astype(F32) + xrecv[1, half, one].astype(F32)
                acc = (acc + own[half, one].astype(F32)).astype(BF)
                if half == 0:
                    otb[2 * one + h] = acc
                else:
                    fin[one] = acc
                    back(one, 0).start()
                    back(one, 1).start()

    order = []
    hooks = {}

    def add(qs, rows, halves):
        for r in rows:
            order.extend([(qs, r, half) for half in halves])

    def hook(fn):
        hooks.setdefault(len(order), []).append(fn)

    def a_wait():
        for i in range(2):
            a_send(i).wait_recv()

    add((0,), (0, 1, 2), (0,))
    hook(lambda: y_last(0))
    add((0,), (3,), (0,))
    add((1,), (0, 1, 2), (0,))
    hook(lambda: turn(2, (0, 2)))
    hook(lambda: y_last(1))
    add((1,), (3,), (0,))
    hook(lambda: turn(2, (1, 3)))
    add((2,), (0, 1, 2), (0,))
    hook(a_wait)
    add((0, 1), (0, 1), (1,))
    hook(lambda: turn(3, (0, 2)))
    add((0, 1), (2, 3), (1,))
    add((2,), (0, 1, 2), (1,))
    hook(lambda: y_last(2))
    add((2,), (3,), (1, 0))
    add((3,), (0,), (1, 0))
    hook(lambda: turn(3, (1, 3)))
    add((3,), (1, 2), (1, 0))
    hook(lambda: y_last(3))
    add((3,), (3,), (1, 0))

    stages = ((0, compute), (LAGS[0], pair), (LAGS[1], passed), (LAGS[2], total))
    for n in range(len(order) + stages[-1][0]):
        for fn in hooks.get(n, ()):
            fn()
        for lag, fn in stages:
            if 0 <= n - lag < len(order):
                fn(n - lag, order[n - lag])

    def out_copy(i):
        return pltpu.make_async_copy(otb.at[i], out_hbm.at[i], out_sem.at[i])

    for kk in range(2):
        out_copy(2 * kk + h).start()
    for kk in range(2):
        for i in range(2):
            back_wait(kk, i)
        out_copy(2 * kk + 1 - h).start()

    for b in CHUNKS:
        for i in range(3):
            wz(b, i).wait_send()
            for q in range(4):
                wy(q, b, i).wait_send()
    for i in range(2):
        a_send(i).wait_send()
    sent_z(ust, urecv, 0).wait_send()
    sent_z(pst, precv, 1).wait_send()
    for i in range(1, NY):
        row_copy(i).wait_send()
    for n, unit in enumerate(order):
        yy, half, ks, mine, kk, far = names(unit)

        @pl.when(jnp.logical_and(mine, far != 0))
        def _():
            relay_copy(n, unit, 0).wait_send()
            relay_copy(n, unit, 1).wait_send()

        @pl.when(jnp.logical_not(mine))
        def _():
            mate_copy(n, unit).wait_send()

        @pl.when(jnp.logical_and(jnp.logical_and(mine, far == 0), half == 1))
        def _():
            for j in range(len(unit[0])):
                one = j if len(unit[0]) == 2 else lax.rem(kq(unit[0][0]), 2)
                back(one, 0).wait_send()
                back(one, 1).wait_send()

    for i in range(4):
        out_copy(i).wait()


def shards(query_rows, key_rows, value_rows, log_decay, norm_gain, out_proj):
    vmem = pltpu.VMEM
    dma = pltpu.SemaphoreType.DMA
    anywhere = pl.BlockSpec(memory_space=pl.ANY)
    near = pl.BlockSpec(memory_space=pltpu.VMEM)
    out = pl.pallas_call(
        kernel,
        name="parity_attention",
        out_shape=jax.ShapeDtypeStruct((4, PIECE, TOK), BF),
        in_specs=[anywhere] * 4 + [near] * 2,
        out_specs=anywhere,
        scratch_shapes=[
            vmem((TOK, WIDTH), BF),
            vmem((TOK, WIDTH), BF),
            vmem((TOK, WIDTH), BF),
            vmem((NY, 4, PIECE, WIDTH), BF),
            vmem((2 * TOK, WIDTH), BF),
            vmem((TOK, WIDTH), F32),
            vmem((TOK, HD), F32),
            vmem((HEADS, TOK), F32),
            vmem((NZ, SLOT, HD), BF),
            vmem((NZ, SLOT, HD), BF),
            vmem((NZ, HD, HD), F32),
            vmem((NZ, HD), F32),
            vmem((SLOT, HD), BF),
            vmem((NY, SLOT, HD), BF),
            vmem((NZ, HD, HD), BF),
            vmem((NZ, HD, HD), BF),
            vmem((NY, 2, 4, PIECE, TOK), BF),
            vmem((8, 2, PIECE, TOK), F32),
            vmem((2, NY, 4, CUT, TOK), BF),
            vmem((2, 2, PIECE, TOK), BF),
            vmem((2, 2, 2, PIECE, TOK), BF),
            vmem((2, PIECE, TOK), BF),
            vmem((4, PIECE, TOK), BF),
            dma((4,)),
            dma((4,)),
            dma((4, 3)),
            dma((4, 3)),
            dma((4, 4, 3)),
            dma((4, 4, 3)),
            dma((2,)),
            dma((2,)),
            dma((NY - 1,)),
            dma((NY,)),
            dma((2,)),
            dma((2,)),
            dma((32,)),
            dma((32,)),
            dma((32, 2)),
            dma((32, 2, 2)),
            dma((32,)),
            dma((2, 2)),
            dma((2, 2)),
        ],
        compiler_params=pltpu.CompilerParams(
            collective_id=0, has_side_effects=True, vmem_limit_bytes=56 * 2**20
        ),
        cost_estimate=pl.CostEstimate(flops=8 * 10**9, bytes_accessed=5 * 2**20, transcendentals=2 * 10**6),
    )(query_rows, key_rows, value_rows, out_proj.T, log_decay.T, norm_gain.reshape(HEADS, HD))
    return out.reshape(4 * PIECE, TOK).T


def solution(mesh):
    return jax.shard_map(
        shards,
        mesh=mesh,
        in_specs=(
            P("section", "group"),
            P("section", "group"),
            P("section", "group"),
            P("section", "group"),
            P("group"),
            P("group", "section"),
        ),
        out_specs=P("section", "group"),
        check_vma=False,
    )
```
